32 devices in a mesh: groups: 2 (over y), dp: 4 (over z), chan: 2 (over x), sub: 2 (over core).
Axes of the slice: x: 2, y: 2, z: 4, core: 2. Of those that a mesh axis runs over, the one named last changes fastest.
Arguments:
- features: bfloat16 [192, 128, 1536], P(('groups', 'dp', 'sub'), None, 'chan'), parts along dimension 0, may hold values from -6 to 6
- cotangent: bfloat16 [192, 128, 1536], P(('groups', 'dp', 'sub'), None, 'chan'), parts along dimension 0, may hold values from -0.076171875 to 0.076171875
- snake_alpha: float32 [1536], P('chan'), may hold values from 0.5 to 4
- conv_weight: bfloat16 [1536, 3, 1536], P('dp', None, 'chan'), may hold values from -0.09375 to 0.09375
- lengths: int32 [192], P(('groups', 'dp', 'sub')), parts along dimension 0, may hold values from 1 to 128, as said below
- kept_rows: int32 [16], P(('groups', 'dp', 'sub')), parts along dimension 0, may hold values from 1 to 6, as said below
- sent_rows: int32 [16], P(('groups', 'dp', 'sub')), parts along dimension 0, may hold values from 0 to 6, as said below
Outputs:
- balanced_out: bfloat16 [112, 128, 1536], P(('groups', 'dp', 'sub'), None, 'chan'), parts along dimension 0
- weight_grad: float32 [3072, 3, 1536], P(('groups', 'dp'), None, 'chan'), parts along dimension 0
The draws below stay inside these ranges and needn't reach their ends.
There are 2 independent parts, one for each index of `groups`. The reference program is written for one: setup_inputs(seed, part) draws one part's arguments, and reference() takes and returns one part's arrays. A program takes and returns all parts, laid end to end along the dimension named above; an argument that names none is the same for every part. Nothing has to cross between parts.
Inputs may be any that keep to these rules, and one draw needn't show every extreme that they name: `kept_rows`: each device keeps at least one row; one device keeps 6. kept_rows[h] + sent_rows[p] <= 7 for every device h and its previous device p; some device hands on 6 rows and some none. The first slot of every device has length 128; lengths of empty slots are not read.
All inputs are finite; a program needn't handle non-finite values.
Results may differ from the reference program's by a relative error of at most 0.01.
Values may be sent and summed in bfloat16 or wider, within the bound.
A program may use at most 128 MiB of HBM per device.

```python
import math
import jax
import jax.numpy as jnp
from jax import lax

CHANNEL_COUNT = 1536
KERNEL_TAPS = 3
DILATION_STEP = 3
TIME_STEPS = 128
KEEP = 6
ROWS_IN = 12
MOVE = 6
CAP = 7
ROWS = 96
N_DP = 4
N_SUB = 2


def row_counts(key):
    holders = N_DP * N_SUB
    index = jnp.arange(holders)
    kept = jax.random.randint(jax.random.fold_in(key, 11), (holders,), 1, KEEP + 1)
    kept = jnp.where(index == 0, KEEP, kept)
    kept = jnp.where(index == N_SUB % holders, 1, kept)
    later = jnp.roll(kept, -N_SUB)
    room = KEEP + 1 - later
    uniform_bits = jax.random.randint(jax.random.fold_in(key, 13), (holders,), 0, 1 << 20)
    sent = uniform_bits % (room + 1)
    sent = jnp.where(index == 0, room, sent)
    sent = jnp.where(index == 1, 0, sent)
    return (kept.astype(jnp.int32), sent.astype(jnp.int32))


def draw_kept_rows(key, part):
    return row_counts(key)[0]


def draw_sent_rows(key, part):
    return row_counts(key)[1]


def draw_lengths(key, part):
    total = ROWS_IN * N_DP * N_SUB
    drawn = jax.random.randint(jax.random.fold_in(key, 17), (total,), 1, TIME_STEPS + 1)
    index = jnp.arange(total)
    return jnp.where(index % ROWS_IN == 0, TIME_STEPS, drawn).astype(jnp.int32)


def level_of(rng, extent, shards, smallest, top_value):
    def one(axis_at, shards_of):
        steps = jax.random.uniform(jax.random.fold_in(jax.random.fold_in(rng, 6), axis_at), (shards_of,), jnp.float32, smallest / len(shards), top_value / len(shards))
        return jnp.repeat(jnp.exp(steps), extent[axis_at] // shards_of).reshape((-1,) + (1,) * (len(extent) - axis_at - 1))

    loudness = one(*shards[0])
    for cut in shards[1:]:
        loudness = loudness * one(*cut)
    return loudness


def normal_values(own_key, dims, width, reach, shards=(), kind=jnp.bfloat16):
    entries = jax.random.normal(own_key, dims, jnp.float32) * width
    if len(shards) > 0:
        entries = level_of(own_key, dims, shards, -0.22, 0.18) * entries
    return jnp.clip(entries, min=-reach, max=reach).astype(kind)


def setup_inputs(seed: int = 0, part: int = 0) -> dict:
    key_list = jax.random.split(jax.random.key(seed), 8)
    part_splits = jax.random.split(jax.random.fold_in(key_list[7], part), 8)
    features = normal_values(part_splits[0], (ROWS, TIME_STEPS, CHANNEL_COUNT), 1.0, 6.0, ((0, 8), (2, 2)))
    cotangent = normal_values(part_splits[1], (ROWS, TIME_STEPS, CHANNEL_COUNT), (1.0 / (N_DP * N_SUB * KEEP * TIME_STEPS) ** 0.5), 0.076171875, ((0, 8), (2, 2)))
    snake_alpha = jnp.clip(jnp.exp(math.log(4.0) - 2.0794415 * jax.random.uniform(key_list[2], (CHANNEL_COUNT,), jnp.float32) ** level_of(key_list[2], (CHANNEL_COUNT,), ((0, 2),), -0.2, 0.2)), 0.5, 4.0)
    conv_weight = normal_values(key_list[3], (CHANNEL_COUNT, KERNEL_TAPS, CHANNEL_COUNT), (KERNEL_TAPS * CHANNEL_COUNT) ** -0.5, 0.09375, ((0, 4), (2, 2)))
    lengths = draw_lengths(jax.random.fold_in(jax.random.fold_in(key_list[7], part), 71), part)
    kept_rows = draw_kept_rows(jax.random.fold_in(jax.random.fold_in(key_list[7], part), 71), part)
    sent_rows = draw_sent_rows(jax.random.fold_in(jax.random.fold_in(key_list[7], part), 71), part)
    return {"features": features, "cotangent": cotangent, "snake_alpha": snake_alpha, "conv_weight": conv_weight, "lengths": lengths, "kept_rows": kept_rows, "sent_rows": sent_rows}


def snake_rows(rows, snake_alpha, time_mask):
    values = rows.astype(jnp.float32)
    shaped = values + jnp.sin(snake_alpha * values) ** 2 / snake_alpha
    return (shaped * time_mask[:, :, None]).astype(jnp.bfloat16)


def place_rows(own_part, arrived, own_keep):
    blank_rows = jnp.zeros((MOVE,) + own_part.shape[1:], own_part.dtype)
    buffer = jnp.concatenate([own_part, blank_rows], axis=0)
    buffer = lax.dynamic_update_slice_in_dim(buffer, arrived, own_keep, 0)
    return buffer[:CAP]


def reference(features, cotangent, snake_alpha, conv_weight, lengths, kept_rows, sent_rows):
    holders = N_DP * N_SUB
    feat_dev = features.reshape(holders, ROWS_IN, TIME_STEPS, CHANNEL_COUNT)
    cot_dev = cotangent.reshape(holders, ROWS_IN, TIME_STEPS, CHANNEL_COUNT)
    len_dev = lengths.reshape(holders, ROWS_IN)

    def balance(device):
        before = (device - N_SUB) % holders
        own_keep = kept_rows[device].astype(jnp.int32)
        prev_keep = kept_rows[before].astype(jnp.int32)
        prev_sent = sent_rows[before]
        keep_slots = jnp.arange(KEEP)
        move_slots = jnp.arange(MOVE)
        own_len = jnp.where(keep_slots < own_keep, len_dev[device][:KEEP], 0).astype(jnp.int32)
        moved_len = jnp.where(move_slots < prev_sent, lax.dynamic_slice_in_dim(len_dev[before], prev_keep, MOVE, 0), 0).astype(jnp.int32)
        moved_feat = lax.dynamic_slice_in_dim(feat_dev[before], prev_keep, MOVE, 0)
        moved_cot = lax.dynamic_slice_in_dim(cot_dev[before], prev_keep, MOVE, 0)
        rows_bal = place_rows(feat_dev[device][:KEEP], moved_feat, own_keep)
        cot_bal = place_rows(cot_dev[device][:KEEP], moved_cot, own_keep)
        len_bal = place_rows(own_len, moved_len, own_keep)
        return rows_bal, cot_bal, len_bal

    rows_bal, cot_bal, len_bal = lax.map(balance, jnp.arange(holders, dtype=jnp.int32))
    rows_bal = rows_bal.reshape(holders * CAP, TIME_STEPS, CHANNEL_COUNT)
    cot_bal = cot_bal.reshape(holders * CAP, TIME_STEPS, CHANNEL_COUNT)
    len_bal = len_bal.reshape(holders * CAP)
    time_mask = (jnp.arange(TIME_STEPS)[None, :] < len_bal[:, None]).astype(jnp.float32)
    snake_output = snake_rows(rows_bal, snake_alpha, time_mask)
    padded_input = jnp.pad(snake_output, ((0, 0), (DILATION_STEP, DILATION_STEP), (0, 0)))
    flattened_rows = holders * CAP * TIME_STEPS
    shifted_tap_rows = [padded_input[:, tap_number * DILATION_STEP:tap_number * DILATION_STEP + TIME_STEPS, :].reshape(flattened_rows, CHANNEL_COUNT) for tap_number in range(KERNEL_TAPS)]
    conv_out = jnp.zeros((flattened_rows, CHANNEL_COUNT), jnp.float32)
    for tap_number in range(KERNEL_TAPS):
        conv_out = conv_out + jnp.dot(shifted_tap_rows[tap_number], conv_weight[:, tap_number, :], preferred_element_type=jnp.float32)
    result = (rows_bal.astype(jnp.float32) + conv_out.reshape(holders * CAP, TIME_STEPS, CHANNEL_COUNT)) * time_mask[:, :, None]
    balanced_out = result.astype(jnp.bfloat16)
    cot_mask = jnp.where(time_mask[:, :, None] > 0.0, cot_bal, jnp.zeros_like(cot_bal))
    cot_flat = cot_mask.reshape(holders, CAP * TIME_STEPS, CHANNEL_COUNT)
    tap_dev = [tap.reshape(holders, CAP * TIME_STEPS, CHANNEL_COUNT) for tap in shifted_tap_rows]

    def add_term(running, device):
        products = []
        for tap_number in range(KERNEL_TAPS):
            products.append(jnp.dot(tap_dev[tap_number][device].T, cot_flat[device], preferred_element_type=jnp.float32))
        term = jnp.stack(products, axis=1)
        rounded = lax.optimization_barrier(term.astype(jnp.bfloat16))
        return running + rounded.astype(jnp.float32), None

    weight_grad, unused = lax.scan(add_term, jnp.zeros((CHANNEL_COUNT, KERNEL_TAPS, CHANNEL_COUNT), jnp.float32), jnp.arange(holders, dtype=jnp.int32))
    return balanced_out, weight_grad
```

```python
import functools

import jax
import jax.numpy as jnp
from jax import lax
from jax.experimental import pallas as pl
from jax.experimental.pallas import tpu as pltpu
from jax.sharding import PartitionSpec as P

KERNEL_TAPS = 3
DILATION_STEP = 3


def from_behind(value, axis, by):
    devices = lax.axis_size(axis)
    return lax.ppermute(value, axis, [(i, (i + by) % devices) for i in range(devices)])


def snake_rows(rows, snake_alpha, time_mask):
    values = rows.astype(jnp.float32)
    shaped = values + jnp.sin(snake_alpha * values) ** 2 / snake_alpha
    return (shaped * time_mask[:, :, None]).astype(jnp.bfloat16)


def on_device(features, cotangent, snake_alpha, conv_weight, lengths, kept_rows, sent_rows):
    slots_in = features.shape[0]
    keep_count = slots_in // 2
    capacity = keep_count + 1
    step_total = features.shape[1]
    chan_width = features.shape[2]
    own_keep = kept_rows[0]
    own_sent = sent_rows[0]
    move_slots = jnp.arange(keep_count)
    keep_slots = jnp.arange(keep_count)
    moved_feat = lax.dynamic_slice_in_dim(features, own_keep, keep_count, 0)
    moved_cot = lax.dynamic_slice_in_dim(cotangent, own_keep, keep_count, 0)
    moved_len = jnp.where(
        move_slots < own_sent, lax.dynamic_slice_in_dim(lengths, own_keep, keep_count, 0), 0
    ).astype(jnp.bfloat16)
    arrived_feat, arrived_cot, arrived_len = from_behind(
        (moved_feat, moved_cot, moved_len), "dp", 1
    )

    def place_rows(own_part, arrived):
        blank_rows = jnp.zeros((keep_count,) + own_part.shape[1:], own_part.dtype)
        buffer = jnp.concatenate([own_part, blank_rows], axis=0)
        buffer = lax.dynamic_update_slice_in_dim(buffer, arrived, own_keep, 0)
        return buffer[:capacity]

    own_len = jnp.where(keep_slots < own_keep, lengths[:keep_count], 0)
    rows_bal = place_rows(features[:keep_count], arrived_feat)
    cot_bal = place_rows(cotangent[:keep_count], arrived_cot)
    len_bal = place_rows(own_len, arrived_len.astype(jnp.int32))
    time_mask = (jnp.arange(step_total)[None, :] < len_bal[:, None]).astype(jnp.float32)
    local_act = snake_rows(rows_bal, snake_alpha, time_mask)
    complete_output = lax.all_gather(local_act, "chan", axis=2, tiled=True)
    padded_width = complete_output.shape[2]
    padded_input = jnp.pad(complete_output, ((0, 0), (DILATION_STEP, DILATION_STEP), (0, 0)))
    flattened_rows = capacity * step_total
    shifted_tap_rows = [
        padded_input[
            :, tap_number * DILATION_STEP : tap_number * DILATION_STEP + step_total, :
        ].reshape(flattened_rows, padded_width)
        for tap_number in range(KERNEL_TAPS)
    ]
    running = jnp.zeros((flattened_rows, chan_width), jnp.float32)
    panel_rows = lax.all_gather(conv_weight, "dp", axis=0, tiled=True)
    for tap_number in range(KERNEL_TAPS):
        columns = shifted_tap_rows[tap_number]
        running = running + jnp.dot(
            columns, panel_rows[:, tap_number, :], preferred_element_type=jnp.float32
        )
    result = (
        rows_bal.astype(jnp.float32) + running.reshape(capacity, step_total, chan_width)
    ) * time_mask[:, :, None]
    balanced_out = result.astype(jnp.bfloat16)
    cot_mask = jnp.where(time_mask[:, :, None] > 0.0, cot_bal, jnp.zeros_like(cot_bal)).reshape(
        flattened_rows, chan_width
    )
    products = []
    for tap_number in range(KERNEL_TAPS):
        columns = shifted_tap_rows[tap_number]
        products.append(
            lax.dot_general(
                columns, cot_mask, (((0,), (0,)), ((), ())), preferred_element_type=jnp.float32
            )
        )
    shard_sum = lax.psum_scatter(
        jnp.stack(products, axis=1).astype(jnp.bfloat16), "dp", scatter_dimension=0, tiled=True
    )
    weight_grad = lax.psum(shard_sum, "sub").astype(jnp.float32)
    return (balanced_out, weight_grad)


PI_HIGH = 3.140625
PI_LOW = 9.67653589793e-4
SINE = (-1.0 / 6, 1.0 / 120, -1.0 / 5040, 1.0 / 362880, -1.0 / 39916800)
MESH = pl.DeviceIdType.MESH


def sine_squared(z):
    turns = jnp.floor(z * (1.0 / 3.14159265358979) + 0.5)
    r = (z - turns * PI_HIGH) - turns * PI_LOW
    r2 = r * r
    poly = SINE[4]
    for coefficient in (SINE[3], SINE[2], SINE[1], SINE[0]):
        poly = poly * r2 + coefficient
    s = r + r * (r2 * poly)
    return s * s


def fused_kernel(
    n, feat, cot, alpha, weight, lengths, kept, sent,
    bal, gout,
    act_all, cot3, wg, own, stage, sib_in, rs_in, rs_right, y_buf, out_full, rows_out, rows_in,
    x_send, x_recv, w_send, w_recv, ws_send, ws_recv, w_local,
    g_send, g_recv, r_send, r_recv, rr_recv, f_send, f_recv, o_send, o_recv,
):
    d = lax.axis_index("dp")
    c = lax.axis_index("chan")
    s = lax.axis_index("sub")
    slots, steps, width = feat.shape
    depth = weight.shape[1]
    half_depth = depth // 2
    half = width // 2
    sib = {"sub": 1 - s}

    def remote(src, dst, send_sem, recv_sem, to):
        return pltpu.make_async_remote_copy(
            src_ref=src, dst_ref=dst, send_sem=send_sem, recv_sem=recv_sem,
            device_id=to, device_id_type=MESH,
        )

    right_ring = lax.rem(d + 1, n)
    left_ring = lax.rem(d + n - 1, n)
    barrier = pltpu.get_barrier_semaphore()
    for peer in (sib, {"chan": 1 - c}, {"dp": right_ring}, {"dp": left_ring}):
        pl.semaphore_signal(barrier, inc=1, device_id=peer, device_id_type=MESH)
    pl.semaphore_wait(barrier, 4)

    def w_part(src):
        return wg.at[:, pl.ds(pl.multiple_of(src * depth + s * half_depth, 16), half_depth), :]

    def w_source(way, k):
        return d - k if way == 0 else d + k

    def w_hop(way, k):
        src = w_source(way, k)
        if k == 0:
            ref = weight.at[:, pl.ds(pl.multiple_of(s * half_depth, 16), half_depth), :]
        else:
            ref = w_part(src)
        to = d + 1 if way == 0 else d - 1
        return remote(ref, w_part(src), w_send.at[way, k], w_recv.at[way, k], {"dp": to})

    def w_share(way, k):
        part = w_part(w_source(way, k))
        return remote(part, part, ws_send.at[way, k], ws_recv.at[way, k], sib)

    def w_exists(way, k):
        return d - k >= 0 if way == 0 else d + k <= n - 1

    def w_more(way):
        return d < n - 1 if way == 0 else d > 0

    def w_start():
        for way in range(2):
            @pl.when(w_more(way))
            def _(way=way):
                w_hop(way, 0).start()

    def w_forward(k):
        for way in range(2):
            @pl.when(w_exists(way, k))
            def _(way=way):
                w_hop(way, k - 1).wait_recv()
                w_share(way, k).start()

            if k < n - 1:
                @pl.when(jnp.logical_and(w_exists(way, k), w_more(way)))
                def _(way=way):
                    w_hop(way, k).start()

    own_weight = pltpu.make_async_copy(
        weight, wg.at[:, pl.ds(pl.multiple_of(d * depth, 16), depth), :], w_local
    )

    def w_finish():
        own_weight.wait()
        for k in range(1, n):
            for way in range(2):
                @pl.when(w_exists(way, k))
                def _(way=way, k=k):
                    w_share(way, k).wait_recv()

    w_start()
    own_weight.start()

    filled = kept[0] + sent[0]

    def slot_length(r):
        return jnp.where(r < filled, lengths[r], 0)

    def x_copy(r):
        part = act_all.at[
            pl.ds(pl.multiple_of(r * steps, steps), steps),
            pl.ds(pl.multiple_of(c * width, width), width),
        ]
        return remote(part, part, x_send.at[r], x_recv.at[r], {"chan": 1 - c})

    tile = 128
    time = lax.broadcasted_iota(jnp.int32, (steps, tile), 0)

    def act_row(r, carry):
        mask = time < slot_length(r)
        at = pl.ds(pl.multiple_of(r * steps, steps), steps)
        for j in range(width // tile):
            cols = pl.ds(j * tile, tile)
            x = feat[r, :, cols].astype(jnp.float32)
            a = alpha[:, cols]
            shaped = x + sine_squared(a * x) * (1.0 / a)
            act_all[at, pl.ds(pl.multiple_of(c * width + j * tile, tile), tile)] = jnp.where(
                mask, shaped, 0.0
            ).astype(jnp.bfloat16)
        x_copy(r).start()
        for j in range(width // tile):
            cols = pl.ds(j * tile, tile)
            v = jnp.where(mask, cot[r, :, cols].astype(jnp.float32), 0.0)
            h, at_col = (j * tile) // half, (j * tile) % half
            early = jnp.where(
                time < steps - DILATION_STEP, pltpu.roll(v, steps - DILATION_STEP, 0), 0.0
            )
            late = jnp.where(time >= DILATION_STEP, pltpu.roll(v, DILATION_STEP, 0), 0.0)
            for q, value in enumerate((early, v, late)):
                cot3[h, at, pl.ds(q * half + at_col, tile)] = value.astype(jnp.bfloat16)
        return carry

    lax.fori_loop(0, slots, act_row, 0)

    def chunk(k):
        first = (0, 1, 3, 2)[k]
        return first + c * (3 - 2 * first)

    def g_copy(e):
        return remote(stage.at[e], sib_in.at[e], g_send.at[e], g_recv.at[e], sib)

    def grad(k):
        e = chunk(k)
        lhs = pl.ds(pl.multiple_of(e * depth, 128), depth)
        dims = (((0,), (0,)), ((), ()))
        stage[e] = lax.dot_general(
            act_all[:, lhs], cot3[1 - s], dims, preferred_element_type=jnp.float32
        ).astype(jnp.bfloat16)
        g_copy(e).start()
        own[e] = lax.dot_general(
            act_all[:, lhs], cot3[s], dims, preferred_element_type=jnp.float32
        )

    def r_copy(e, q, way):
        cols = pl.ds(q * half, half)
        src = sib_in.at[e, :, cols]
        if way == 0:
            return remote(src, rs_in.at[e, :, cols], r_send.at[e, q], r_recv.at[e, q], {"dp": d + 1})
        if way == 1:
            return remote(src, rs_in.at[e, :, cols], r_send.at[e, q], r_recv.at[e, q], {"dp": d - 1})
        return remote(src, rs_right.at[:, cols], r_send.at[e, q], rr_recv.at[q], {"dp": d - 1})

    def f_copy(q):
        cols = pl.ds(pl.multiple_of(s * half, half), half)
        part = gout.at[q, :, cols]
        return remote(part, part, f_send.at[q], f_recv.at[q], sib)

    def reduce_step(k, q):
        e = chunk(k)
        cols = pl.ds(q * half, half)
        if q == 0:
            g_copy(e).wait_recv()
        enters = jnp.logical_or(
            jnp.logical_and(d <= e, d > 0), jnp.logical_and(d > e, d < n - 1)
        )

        @pl.when(enters)
        def _():
            r_copy(e, q, 0).wait_recv()
            own[e, :, cols] = own[e, :, cols] + rs_in[e, :, cols].astype(jnp.float32)

        @pl.when(jnp.logical_and(d == e, d < n - 1))
        def _():
            r_copy(e, q, 2).wait_recv()
            own[e, :, cols] = own[e, :, cols] + rs_right[:, cols].astype(jnp.float32)

        total = own[e, :, cols] + sib_in[e, :, cols].astype(jnp.float32)

        @pl.when(d != e)
        def _():
            sib_in[e, :, cols] = total.astype(jnp.bfloat16)

        @pl.when(d < e)
        def _():
            r_copy(e, q, 0).start()

        @pl.when(d > e + 1)
        def _():
            r_copy(e, q, 1).start()

        @pl.when(d == e + 1)
        def _():
            r_copy(e, q, 2).start()

        @pl.when(d == e)
        def _():
            gout[q, :, pl.ds(pl.multiple_of(s * half, half), half)] = total
            f_copy(q).start()

    group = y_buf.shape[1] // steps

    def conv(g):
        at = pl.ds(g * group * steps, group * steps)
        for q in range(KERNEL_TAPS):
            y_buf[q] = jnp.dot(act_all[at, :], wg[q], preferred_element_type=jnp.float32)

        def finish(i, carry):
            r = g * group + i
            mask = time < slot_length(r)
            rows = pl.ds(pl.multiple_of(i * steps, steps), steps)
            for j in range(width // tile):
                cols = pl.ds(j * tile, tile)
                before = jnp.where(
                    time >= DILATION_STEP, pltpu.roll(y_buf[0, rows, cols], DILATION_STEP, 0), 0.0
                )
                after = jnp.where(
                    time < steps - DILATION_STEP,
                    pltpu.roll(y_buf[2, rows, cols], steps - DILATION_STEP, 0),
                    0.0,
                )
                value = feat[r, :, cols].astype(jnp.float32) + (before + y_buf[1, rows, cols] + after)
                out_full[r, :, cols] = jnp.where(mask, value, 0.0).astype(jnp.bfloat16)
            return carry

        lax.fori_loop(0, group, finish, 0)

    grad(0)
    grad(1)
    w_forward(1)
    for q in range(KERNEL_TAPS):
        reduce_step(0, q)
    for r in range(slots):
        x_copy(r).wait_recv()
    w_forward(2)
    grad(2)
    grad(3)
    for q in range(KERNEL_TAPS):
        reduce_step(1, q)
    w_forward(3)
    w_finish()
    groups = slots // group
    conv(0)
    for q in range(KERNEL_TAPS):
        reduce_step(2, q)
    for g in range(1, groups):
        conv(g)
    own_keep = kept[0]
    moved = rows_out.shape[0]
    for j in range(moved):
        rows_out[j] = out_full[own_keep + j]
    o_copy = remote(rows_out, rows_in, o_send, o_recv, {"dp": right_ring})
    o_copy.start()
    for q in range(KERNEL_TAPS):
        reduce_step(3, q)
    o_copy.wait_recv()
    for j in range(bal.shape[0]):
        arrived = rows_in[jnp.clip(j - own_keep, 0, moved - 1)]
        if j < moved:
            bal[j] = jnp.where(j < own_keep, out_full[j], arrived)
        else:
            bal[j] = arrived
    for q in range(KERNEL_TAPS):
        f_copy(q).wait_recv()

    for r in range(slots):
        x_copy(r).wait_send()
    for way in range(2):
        for k in range(n):
            if k < n - 1:
                @pl.when(jnp.logical_and(w_exists(way, k), w_more(way)))
                def _(way=way, k=k):
                    w_hop(way, k).wait_send()
            if k > 0:
                @pl.when(w_exists(way, k))
                def _(way=way, k=k):
                    w_share(way, k).wait_send()
    for k in range(n):
        e = chunk(k)
        g_copy(e).wait_send()

        @pl.when(d != e)
        def _(e=e):
            for q in range(KERNEL_TAPS):
                r_copy(e, q, 0).wait_send()
    for q in range(KERNEL_TAPS):
        f_copy(q).wait_send()
    o_copy.wait_send()


def fused_on_device(features, cotangent, snake_alpha, conv_weight, lengths, kept_rows, sent_rows):
    n = lax.axis_size("dp")
    slots, steps, width = features.shape
    depth = conv_weight.shape[0]
    total = 2 * width
    moved = slots // 2
    group = 4
    bf16, f32 = jnp.bfloat16, jnp.float32
    vmem = pl.BlockSpec(memory_space=pltpu.VMEM)
    smem = pl.BlockSpec(memory_space=pltpu.SMEM)
    dma = pltpu.SemaphoreType.DMA
    wide = KERNEL_TAPS * width // 2
    weight = jnp.transpose(conv_weight, (1, 0, 2))
    flops = 2 * 2 * slots * steps * total * KERNEL_TAPS * width
    bal, gout = pl.pallas_call(
        functools.partial(fused_kernel, n),
        out_shape=(
            jax.ShapeDtypeStruct((moved + 1, steps, width), bf16),
            jax.ShapeDtypeStruct((KERNEL_TAPS, depth, width), f32),
        ),
        in_specs=[vmem] * 4 + [smem] * 3,
        out_specs=(vmem, vmem),
        scratch_shapes=[
            pltpu.VMEM((slots * steps, total), bf16),
            pltpu.VMEM((2, slots * steps, wide), bf16),
            pltpu.VMEM((KERNEL_TAPS, total, width), bf16),
            pltpu.VMEM((n, depth, wide), f32),
            pltpu.VMEM((n, depth, wide), bf16),
            pltpu.VMEM((n, depth, wide), bf16),
            pltpu.VMEM((n, depth, wide), bf16),
            pltpu.VMEM((depth, wide), bf16),
            pltpu.VMEM((KERNEL_TAPS, group * steps, width), f32),
            pltpu.VMEM((slots, steps, width), bf16),
            pltpu.VMEM((moved, steps, width), bf16),
            pltpu.VMEM((moved, steps, width), bf16),
            dma((slots,)), dma((slots,)),
            dma((2, n)), dma((2, n)), dma((2, n)), dma((2, n)), dma,
            dma((n,)), dma((n,)), dma((n, KERNEL_TAPS)), dma((n, KERNEL_TAPS)), dma((KERNEL_TAPS,)),
            dma((KERNEL_TAPS,)), dma((KERNEL_TAPS,)), dma, dma,
        ],
        compiler_params=pltpu.CompilerParams(
            collective_id=0, has_side_effects=True, vmem_limit_bytes=63 * 1024 * 1024
        ),
        cost_estimate=pl.CostEstimate(flops=flops, bytes_accessed=16 * 2**20, transcendentals=0),
        name="snake_conv_fused",
    )(features, cotangent, snake_alpha[None, :], weight, lengths, kept_rows, sent_rows)
    return bal, jnp.transpose(gout, (1, 0, 2))


def solution(mesh):
    placed = (
        P(("groups", "dp", "sub"), None, "chan"),
        P(("groups", "dp", "sub"), None, "chan"),
        P("chan"),
        P("dp", None, "chan"),
        P(("groups", "dp", "sub")),
        P(("groups", "dp", "sub")),
        P(("groups", "dp", "sub")),
    )
    fits = mesh.shape["dp"] == 4 and mesh.shape["chan"] == 2
    return jax.shard_map(
        fused_on_device if fits else on_device,
        mesh=mesh,
        in_specs=placed,
        out_specs=(P(("groups", "dp", "sub"), None, "chan"), P(("groups", "dp"), None, "chan")),
        check_vma=False,
    )
```

```python
import functools

import jax
import jax.numpy as jnp
from jax import lax
from jax.experimental import pallas as pl
from jax.experimental.pallas import tpu as pltpu
from jax.sharding import PartitionSpec as P

KERNEL_TAPS = 3
DILATION_STEP = 3


def from_behind(value, axis, by):
    devices = lax.axis_size(axis)
    return lax.ppermute(value, axis, [(i, (i + by) % devices) for i in range(devices)])


def snake_rows(rows, snake_alpha, time_mask):
    values = rows.astype(jnp.float32)
    shaped = values + jnp.sin(snake_alpha * values) ** 2 / snake_alpha
    return (shaped * time_mask[:, :, None]).astype(jnp.bfloat16)


def on_device(features, cotangent, snake_alpha, conv_weight, lengths, kept_rows, sent_rows):
    slots_in = features.shape[0]
    keep_count = slots_in // 2
    capacity = keep_count + 1
    step_total = features.shape[1]
    chan_width = features.shape[2]
    own_keep = kept_rows[0]
    own_sent = sent_rows[0]
    move_slots = jnp.arange(keep_count)
    keep_slots = jnp.arange(keep_count)
    moved_feat = lax.dynamic_slice_in_dim(features, own_keep, keep_count, 0)
    moved_cot = lax.dynamic_slice_in_dim(cotangent, own_keep, keep_count, 0)
    moved_len = jnp.where(
        move_slots < own_sent, lax.dynamic_slice_in_dim(lengths, own_keep, keep_count, 0), 0
    ).astype(jnp.bfloat16)
    arrived_feat, arrived_cot, arrived_len = from_behind(
        (moved_feat, moved_cot, moved_len), "dp", 1
    )

    def place_rows(own_part, arrived):
        blank_rows = jnp.zeros((keep_count,) + own_part.shape[1:], own_part.dtype)
        buffer = jnp.concatenate([own_part, blank_rows], axis=0)
        buffer = lax.dynamic_update_slice_in_dim(buffer, arrived, own_keep, 0)
        return buffer[:capacity]

    own_len = jnp.where(keep_slots < own_keep, lengths[:keep_count], 0)
    rows_bal = place_rows(features[:keep_count], arrived_feat)
    cot_bal = place_rows(cotangent[:keep_count], arrived_cot)
    len_bal = place_rows(own_len, arrived_len.astype(jnp.int32))
    time_mask = (jnp.arange(step_total)[None, :] < len_bal[:, None]).astype(jnp.float32)
    local_act = snake_rows(rows_bal, snake_alpha, time_mask)
    complete_output = lax.all_gather(local_act, "chan", axis=2, tiled=True)
    padded_width = complete_output.shape[2]
    padded_input = jnp.pad(complete_output, ((0, 0), (DILATION_STEP, DILATION_STEP), (0, 0)))
    flattened_rows = capacity * step_total
    shifted_tap_rows = [
        padded_input[
            :, tap_number * DILATION_STEP : tap_number * DILATION_STEP + step_total, :
        ].reshape(flattened_rows, padded_width)
        for tap_number in range(KERNEL_TAPS)
    ]
    running = jnp.zeros((flattened_rows, chan_width), jnp.float32)
    panel_rows = lax.all_gather(conv_weight, "dp", axis=0, tiled=True)
    for tap_number in range(KERNEL_TAPS):
        columns = shifted_tap_rows[tap_number]
        running = running + jnp.dot(
            columns, panel_rows[:, tap_number, :], preferred_element_type=jnp.float32
        )
    result = (
        rows_bal.astype(jnp.float32) + running.reshape(capacity, step_total, chan_width)
    ) * time_mask[:, :, None]
    balanced_out = result.astype(jnp.bfloat16)
    cot_mask = jnp.where(time_mask[:, :, None] > 0.0, cot_bal, jnp.zeros_like(cot_bal)).reshape(
        flattened_rows, chan_width
    )
    products = []
    for tap_number in range(KERNEL_TAPS):
        columns = shifted_tap_rows[tap_number]
        products.append(
            lax.dot_general(
                columns, cot_mask, (((0,), (0,)), ((), ())), preferred_element_type=jnp.float32
            )
        )
    shard_sum = lax.psum_scatter(
        jnp.stack(products, axis=1).astype(jnp.bfloat16), "dp", scatter_dimension=0, tiled=True
    )
    weight_grad = lax.psum(shard_sum, "sub").astype(jnp.float32)
    return (balanced_out, weight_grad)


PI_HIGH = 3.140625
PI_LOW = 9.67653589793e-4
SINE = (-1.0 / 6, 1.0 / 120, -1.0 / 5040, 1.0 / 362880, -1.0 / 39916800)
MESH = pl.DeviceIdType.MESH


def sine_squared(z):
    turns = jnp.floor(z * (1.0 / 3.14159265358979) + 0.5)
    r = (z - turns * PI_HIGH) - turns * PI_LOW
    r2 = r * r
    poly = SINE[4]
    for coefficient in (SINE[3], SINE[2], SINE[1], SINE[0]):
        poly = poly * r2 + coefficient
    s = r + r * (r2 * poly)
    return s * s


def fused_kernel(
    n, feat, cot, alpha, weight, lengths, kept, sent,
    bal, gout,
    act_all, cot3, wg, own, stage, sib_in, rs_in, rs_right, y_buf, out_full, rows_out, rows_in,
    x_send, x_recv, w_send, w_recv, ws_send, ws_recv, wy_send, wy_recv, wr_send, wr_recv, w_local,
    g_send, g_recv, r_send, r_recv, rr_recv, f_send, f_recv, o_send, o_recv,
):
    d = lax.axis_index("dp")
    c = lax.axis_index("chan")
    s = lax.axis_index("sub")
    y = lax.axis_index("groups")
    slots, steps, width = feat.shape
    depth = weight.shape[1]
    quarter = depth // 4
    half = width // 2
    sib = {"sub": 1 - s}
    across = {"groups": 1 - y}

    def remote(src, dst, send_sem, recv_sem, to):
        return pltpu.make_async_remote_copy(
            src_ref=src, dst_ref=dst, send_sem=send_sem, recv_sem=recv_sem,
            device_id=to, device_id_type=MESH,
        )

    right_ring = lax.rem(d + 1, n)
    left_ring = lax.rem(d + n - 1, n)
    barrier = pltpu.get_barrier_semaphore()
    for peer in (sib, across, {"chan": 1 - c}, {"dp": right_ring}, {"dp": left_ring}):
        pl.semaphore_signal(barrier, inc=1, device_id=peer, device_id_type=MESH)
    pl.semaphore_wait(barrier, 5)

    def w_part(src, group):
        at = src * depth + (2 * group + s) * quarter
        return wg.at[:, pl.ds(pl.multiple_of(at, 16), quarter), :]

    def w_source(way, k):
        return d - k if way == 0 else d + k

    def w_hop(way, k):
        src = w_source(way, k)
        if k == 0:
            ref = weight.at[:, pl.ds(pl.multiple_of((2 * y + s) * quarter, 16), quarter), :]
        else:
            ref = w_part(src, y)
        to = d + 1 if way == 0 else d - 1
        return remote(ref, w_part(src, y), w_send.at[way, k], w_recv.at[way, k], {"dp": to})

    def w_share(way, k):
        part = w_part(w_source(way, k), y)
        return remote(part, part, ws_send.at[way, k], ws_recv.at[way, k], sib)

    def w_cross(way, k):
        part = w_part(w_source(way, k), y)
        return remote(part, part, wy_send.at[way, k], wy_recv.at[way, k], across)

    def w_pass(way, k):
        part = w_part(w_source(way, k), 1 - y)
        return remote(part, part, wr_send.at[way, k], wr_recv.at[way, k], sib)

    def w_exists(way, k):
        return d - k >= 0 if way == 0 else d + k <= n - 1

    def w_more(way):
        return d < n - 1 if way == 0 else d > 0

    def w_start():
        for way in range(2):
            @pl.when(w_more(way))
            def _(way=way):
                w_hop(way, 0).start()

    def w_forward(k):
        for way in range(2):
            @pl.when(w_exists(way, k))
            def _(way=way):
                w_hop(way, k - 1).wait_recv()
                w_cross(way, k).start()
                w_share(way, k).start()

            if k < n - 1:
                @pl.when(jnp.logical_and(w_exists(way, k), w_more(way)))
                def _(way=way):
                    w_hop(way, k).start()

    def w_relay(k):
        for way in range(2):
            @pl.when(w_exists(way, k))
            def _(way=way):
                w_cross(way, k).wait_recv()
                w_pass(way, k).start()

    own_weight = pltpu.make_async_copy(
        weight, wg.at[:, pl.ds(pl.multiple_of(d * depth, 16), depth), :], w_local
    )

    def w_finish():
        own_weight.wait()
        for k in range(1, n):
            for way in range(2):
                @pl.when(w_exists(way, k))
                def _(way=way, k=k):
                    w_share(way, k).wait_recv()
                    w_pass(way, k).wait_recv()

    w_start()
    own_weight.start()

    filled = kept[0] + sent[0]

    def slot_length(r):
        return jnp.where(r < filled, lengths[r], 0)

    def x_copy(r):
        part = act_all.at[
            pl.ds(pl.multiple_of(r * steps, steps), steps),
            pl.ds(pl.multiple_of(c * width, width), width),
        ]
        return remote(part, part, x_send.at[r], x_recv.at[r], {"chan": 1 - c})

    tile = 128
    time = lax.broadcasted_iota(jnp.int32, (steps, tile), 0)

    def act_row(r, carry):
        mask = time < slot_length(r)
        at = pl.ds(pl.multiple_of(r * steps, steps), steps)
        for j in range(width // tile):
            cols = pl.ds(j * tile, tile)
            x = feat[r, :, cols].astype(jnp.float32)
            a = alpha[:, cols]
            shaped = x + sine_squared(a * x) * (1.0 / a)
            act_all[at, pl.ds(pl.multiple_of(c * width + j * tile, tile), tile)] = jnp.where(
                mask, shaped, 0.0
            ).astype(jnp.bfloat16)
        x_copy(r).start()
        for j in range(width // tile):
            cols = pl.ds(j * tile, tile)
            v = jnp.where(mask, cot[r, :, cols].astype(jnp.float32), 0.0)
            h, at_col = (j * tile) // half, (j * tile) % half
            early = jnp.where(
                time < steps - DILATION_STEP, pltpu.roll(v, steps - DILATION_STEP, 0), 0.0
            )
            late = jnp.where(time >= DILATION_STEP, pltpu.roll(v, DILATION_STEP, 0), 0.0)
            for q, value in enumerate((early, v, late)):
                cot3[h, at, pl.ds(q * half + at_col, tile)] = value.astype(jnp.bfloat16)
        return carry

    lax.fori_loop(0, slots, act_row, 0)

    def chunk(k):
        first = (0, 1, 3, 2)[k]
        return first + c * (3 - 2 * first)

    def g_copy(e):
        return remote(stage.at[e], sib_in.at[e], g_send.at[e], g_recv.at[e], sib)

    def grad(k):
        e = chunk(k)
        lhs = pl.ds(pl.multiple_of(e * depth, 128), depth)
        dims = (((0,), (0,)), ((), ()))
        stage[e] = lax.dot_general(
            act_all[:, lhs], cot3[1 - s], dims, preferred_element_type=jnp.float32
        ).astype(jnp.bfloat16)
        g_copy(e).start()
        own[e] = lax.dot_general(
            act_all[:, lhs], cot3[s], dims, preferred_element_type=jnp.float32
        )

    def r_copy(e, q, way):
        cols = pl.ds(q * half, half)
        src = sib_in.at[e, :, cols]
        if way == 0:
            return remote(src, rs_in.at[e, :, cols], r_send.at[e, q], r_recv.at[e, q], {"dp": d + 1})
        if way == 1:
            return remote(src, rs_in.at[e, :, cols], r_send.at[e, q], r_recv.at[e, q], {"dp": d - 1})
        return remote(src, rs_right.at[:, cols], r_send.at[e, q], rr_recv.at[q], {"dp": d - 1})

    def f_copy(q):
        cols = pl.ds(pl.multiple_of(s * half, half), half)
        part = gout.at[q, :, cols]
        return remote(part, part, f_send.at[q], f_recv.at[q], sib)

    def starts_chain(e):
        return jnp.logical_or(
            jnp.logical_and(d < e, d == 0), jnp.logical_and(d > e, d == n - 1)
        )

    def first_steps(k):
        @pl.when(starts_chain(chunk(k)))
        def _():
            for q in range(KERNEL_TAPS):
                reduce_step(k, q)

    def next_step(k, q):
        @pl.when(jnp.logical_not(starts_chain(chunk(k))))
        def _():
            reduce_step(k, q)

    def reduce_step(k, q):
        e = chunk(k)
        cols = pl.ds(q * half, half)
        if q == 0:
            g_copy(e).wait_recv()
        enters = jnp.logical_or(
            jnp.logical_and(d <= e, d > 0), jnp.logical_and(d > e, d < n - 1)
        )

        @pl.when(enters)
        def _():
            r_copy(e, q, 0).wait_recv()
            own[e, :, cols] = own[e, :, cols] + rs_in[e, :, cols].astype(jnp.float32)

        @pl.when(jnp.logical_and(d == e, d < n - 1))
        def _():
            r_copy(e, q, 2).wait_recv()
            own[e, :, cols] = own[e, :, cols] + rs_right[:, cols].astype(jnp.float32)

        total = own[e, :, cols] + sib_in[e, :, cols].astype(jnp.float32)

        @pl.when(d != e)
        def _():
            sib_in[e, :, cols] = total.astype(jnp.bfloat16)

        @pl.when(d < e)
        def _():
            r_copy(e, q, 0).start()

        @pl.when(d > e + 1)
        def _():
            r_copy(e, q, 1).start()

        @pl.when(d == e + 1)
        def _():
            r_copy(e, q, 2).start()

        @pl.when(d == e)
        def _():
            gout[q, :, pl.ds(pl.multiple_of(s * half, half), half)] = total
            f_copy(q).start()

    group = y_buf.shape[1] // steps

    def conv(g):
        at = pl.ds(g * group * steps, group * steps)
        for q in range(KERNEL_TAPS):
            y_buf[q] = jnp.dot(act_all[at, :], wg[q], preferred_element_type=jnp.float32)

        def finish(i, carry):
            r = g * group + i
            mask = time < slot_length(r)
            rows = pl.ds(pl.multiple_of(i * steps, steps), steps)
            for j in range(width // tile):
                cols = pl.ds(j * tile, tile)
                before = jnp.where(
                    time >= DILATION_STEP, pltpu.roll(y_buf[0, rows, cols], DILATION_STEP, 0), 0.0
                )
                after = jnp.where(
                    time < steps - DILATION_STEP,
                    pltpu.roll(y_buf[2, rows, cols], steps - DILATION_STEP, 0),
                    0.0,
                )
                value = feat[r, :, cols].astype(jnp.float32) + (before + y_buf[1, rows, cols] + after)
                out_full[r, :, cols] = jnp.where(mask, value, 0.0).astype(jnp.bfloat16)
            return carry

        lax.fori_loop(0, group, finish, 0)

    grad(0)
    grad(1)
    first_steps(0)
    first_steps(1)
    w_forward(1)
    next_step(0, 0)
    w_relay(1)
    w_forward(2)
    for r in range(slots):
        x_copy(r).wait_recv()
    grad(2)
    first_steps(2)
    grad(3)
    first_steps(3)
    next_step(0, 1)
    w_relay(2)
    w_forward(3)
    next_step(0, 2)
    w_relay(3)
    next_step(1, 0)
    w_finish()
    conv(0)
    next_step(2, 0)
    conv(1)
    next_step(1, 1)
    conv(2)
    own_keep = kept[0]
    moved = rows_out.shape[0]
    for j in range(moved):
        rows_out[j] = out_full[own_keep + j]
    o_copy = remote(rows_out, rows_in, o_send, o_recv, {"dp": right_ring})
    o_copy.start()
    next_step(2, 1)
    next_step(1, 2)
    next_step(2, 2)
    for q in range(KERNEL_TAPS):
        next_step(3, q)
    o_copy.wait_recv()
    for j in range(bal.shape[0]):
        arrived = rows_in[jnp.clip(j - own_keep, 0, moved - 1)]
        if j < moved:
            bal[j] = jnp.where(j < own_keep, out_full[j], arrived)
        else:
            bal[j] = arrived
    for q in range(KERNEL_TAPS):
        f_copy(q).wait_recv()

    for r in range(slots):
        x_copy(r).wait_send()
    for way in range(2):
        for k in range(n):
            if k < n - 1:
                @pl.when(jnp.logical_and(w_exists(way, k), w_more(way)))
                def _(way=way, k=k):
                    w_hop(way, k).wait_send()
            if k > 0:
                @pl.when(w_exists(way, k))
                def _(way=way, k=k):
                    w_share(way, k).wait_send()
                    w_cross(way, k).wait_send()
                    w_pass(way, k).wait_send()
    for k in range(n):
        e = chunk(k)
        g_copy(e).wait_send()

        @pl.when(d != e)
        def _(e=e):
            for q in range(KERNEL_TAPS):
                r_copy(e, q, 0).wait_send()
    for q in range(KERNEL_TAPS):
        f_copy(q).wait_send()
    o_copy.wait_send()


def fused_on_device(features, cotangent, snake_alpha, conv_weight, lengths, kept_rows, sent_rows):
    n = lax.axis_size("dp")
    slots, steps, width = features.shape
    depth = conv_weight.shape[0]
    total = 2 * width
    moved = slots // 2
    group = 4
    bf16, f32 = jnp.bfloat16, jnp.float32
    vmem = pl.BlockSpec(memory_space=pltpu.VMEM)
    smem = pl.BlockSpec(memory_space=pltpu.SMEM)
    dma = pltpu.SemaphoreType.DMA
    wide = KERNEL_TAPS * width // 2
    weight = jnp.transpose(conv_weight, (1, 0, 2))
    flops = 2 * 2 * slots * steps * total * KERNEL_TAPS * width
    bal, gout = pl.pallas_call(
        functools.partial(fused_kernel, n),
        out_shape=(
            jax.ShapeDtypeStruct((moved + 1, steps, width), bf16),
            jax.ShapeDtypeStruct((KERNEL_TAPS, depth, width), f32),
        ),
        in_specs=[vmem] * 4 + [smem] * 3,
        out_specs=(vmem, vmem),
        scratch_shapes=[
            pltpu.VMEM((slots * steps, total), bf16),
            pltpu.VMEM((2, slots * steps, wide), bf16),
            pltpu.VMEM((KERNEL_TAPS, total, width), bf16),
            pltpu.VMEM((n, depth, wide), f32),
            pltpu.VMEM((n, depth, wide), bf16),
            pltpu.VMEM((n, depth, wide), bf16),
            pltpu.VMEM((n, depth, wide), bf16),
            pltpu.VMEM((depth, wide), bf16),
            pltpu.VMEM((KERNEL_TAPS, group * steps, width), f32),
            pltpu.VMEM((slots, steps, width), bf16),
            pltpu.VMEM((moved, steps, width), bf16),
            pltpu.VMEM((moved, steps, width), bf16),
            dma((slots,)), dma((slots,)),
            *[dma((2, n))] * 8, dma,
            dma((n,)), dma((n,)), dma((n, KERNEL_TAPS)), dma((n, KERNEL_TAPS)), dma((KERNEL_TAPS,)),
            dma((KERNEL_TAPS,)), dma((KERNEL_TAPS,)), dma, dma,
        ],
        compiler_params=pltpu.CompilerParams(
            collective_id=0, has_side_effects=True, vmem_limit_bytes=63 * 1024 * 1024
        ),
        cost_estimate=pl.CostEstimate(flops=flops, bytes_accessed=16 * 2**20, transcendentals=0),
        name="snake_conv_fused",
    )(features, cotangent, snake_alpha[None, :], weight, lengths, kept_rows, sent_rows)
    return bal, jnp.transpose(gout, (1, 0, 2))


def solution(mesh):
    placed = (
        P(("groups", "dp", "sub"), None, "chan"),
        P(("groups", "dp", "sub"), None, "chan"),
        P("chan"),
        P("dp", None, "chan"),
        P(("groups", "dp", "sub")),
        P(("groups", "dp", "sub")),
        P(("groups", "dp", "sub")),
    )
    fits = mesh.shape["dp"] == 4 and mesh.shape["chan"] == 2
    fits = fits and mesh.shape["groups"] == 2
    return jax.shard_map(
        fused_on_device if fits else on_device,
        mesh=mesh,
        in_specs=placed,
        out_specs=(P(("groups", "dp", "sub"), None, "chan"), P(("groups", "dp"), None, "chan")),
        check_vma=False,
    )
```
